32 devices in a mesh: seq: 4 (over y, x), rep: 8 (over z, core).
Axes of the slice: x: 2, y: 2, z: 4, core: 2. Of those that a mesh axis runs over, the one named last changes fastest.
Arguments:
- mixer_in: bfloat16 [8, 512, 4096], P('rep', 'seq'), may hold values from -6 to 6
- write_proj: bfloat16 [8, 512, 512], P('rep', 'seq'), may hold values from -6 to 6
- read_proj: bfloat16 [8, 512, 512], P('rep', 'seq'), may hold values from -0.5 to 0.5
- dt_steps: int32 [8, 512, 64], P('rep', 'seq'), may hold values from 1 to 16
- decay_exp: int32 [8, 512, 64], P('rep', 'seq'), may hold values from 1 to 50000, as said below
- norm_gain: float32 [4096], P('seq'), may hold values from 0.1 to 1.9
- skip_gain: float32 [64], P('seq'), may hold values from 1 to 4
- out_grad: bfloat16 [8, 512, 4096], P('rep', 'seq'), may hold values from -80 to 80
Outputs:
- mixer_grad: bfloat16 [8, 512, 4096], P('rep', 'seq')
- read_grad: bfloat16 [8, 512, 512], P('rep', 'seq')
- gain_grad: float32 [4096], P('seq')
- skip_grad: float32 [64], P('seq')
The draws below stay inside these ranges and needn't reach their ends.
Inputs may be any that keep to these rules, and one draw needn't show every extreme that they name: The decay factor of head h at position t is exp(-decay_exp / 65536).
All inputs are finite; a program needn't handle non-finite values.
Results may differ from the reference program's by a relative error of at most 0.015.
Values may be sent and summed in bfloat16 or wider, within the bound.
A program may use at most 64 MiB of HBM per device.

```python
from functools import partial
import jax
import jax.numpy as jnp
from jax import lax

H = 64
P_SIZE = 64
N = 128
G = 4
HG = 16
L_DEV = 128
SEQLEN = 512
BATCH = 8
N_SEQ = 4


def draw_decay_exp(key, part):
    keys = jax.random.split(key, 8)
    blocks = SEQLEN // L_DEV
    mixed_group = jax.random.randint(keys[0], (BATCH, 1, G, 1), 0, 2)
    mixed_head = jnp.broadcast_to(mixed_group, (BATCH, 1, G, HG)).reshape(BATCH, 1, 1, H)
    quick_turn = jax.random.randint(keys[7], (BATCH, blocks, 1, H), 0, 3)
    quick_block = mixed_head * (quick_turn == 0).astype(jnp.int32)
    slow_unit = max(32768 // SEQLEN // 6, 1)
    magnitude = jax.random.randint(keys[1], (BATCH, blocks, 1, H), 1, 5)
    quick_factor = 1 + (magnitude + 1) // 2
    per_block = jnp.where(quick_block == 1, 256 * quick_factor, slow_unit * magnitude)
    per_block = jnp.broadcast_to(per_block, (BATCH, blocks, L_DEV, H)).reshape(BATCH, SEQLEN, H)
    stochastic_perturbation = jax.random.randint(keys[2], (BATCH, SEQLEN, H), 1, 5)
    front_displacement = jax.random.randint(keys[3], (BATCH, 1, H), 0, SEQLEN // 2)
    rear_displacement = jax.random.randint(keys[4], (BATCH, 1, H), SEQLEN // 2, SEQLEN)
    front_extent = jax.random.randint(keys[5], (BATCH, 1, H), 14600, 45400)
    rear_extent = jax.random.randint(keys[6], (BATCH, 1, H), 14600, 45400)
    element_indices = jnp.arange(SEQLEN)[None, :, None]
    pulse_clusters = jnp.where(element_indices == front_displacement, front_extent, 0) + jnp.where(element_indices == rear_displacement, rear_extent, 0)
    pulse_clusters = pulse_clusters * (1 - mixed_head.reshape(BATCH, 1, H))
    return (per_block * stochastic_perturbation + pulse_clusters).astype(jnp.int32)


def draw_out_grad(key, part):
    position = jnp.arange(SEQLEN, dtype=jnp.float32) / SEQLEN
    sequence = jnp.arange(BATCH, dtype=jnp.float32) / BATCH
    scale = (1.0 + 2.0 * position)[None, :, None] * (1.0 + 2.0 * sequence)[:, None, None]
    values = jnp.clip(jax.random.normal(key, (BATCH, SEQLEN, H * P_SIZE), jnp.float32), -4.0, 4.0) * scale
    return values.astype(jnp.bfloat16)


def plant(array, stream_key, smallest, largest):
    extent = array.shape
    place = [jax.random.randint(jax.random.fold_in(stream_key, axis), (), 0, extent[axis]) for axis in range(len(extent))]
    array = array.at[tuple(place)].set(smallest)
    longest = extent.index(max(extent))
    place[longest] = (place[longest] + 1) % extent[longest]
    return array.at[tuple(place)].set(largest)


def block_levels(stream_key, extent, cuts, low, high):
    factor_of = 1.0
    for dim, shards_of in cuts:
        heights = jax.random.uniform(jax.random.fold_in(jax.random.fold_in(stream_key, 6), dim), (shards_of,), jnp.float32, low / len(cuts), high / len(cuts))
        factor_of = factor_of * jnp.repeat(jnp.exp(heights), extent[dim] // shards_of).reshape((-1,) + (1,) * (len(extent) - 1 - dim))
    return factor_of


def gaussian(own_key, shape, deviation, reach, cuts=(), kind=jnp.bfloat16):
    values = jax.random.normal(own_key, shape, jnp.float32) * deviation
    if len(cuts) > 0:
        values = block_levels(own_key, shape, cuts, -0.22, 0.18) * values
    return jnp.clip(values, min=-reach, max=reach).astype(kind)


def setup_inputs(seed: int = 0) -> dict:
    arg_keys = jax.random.split(jax.random.key(seed), 9)
    return {
        "mixer_in": gaussian(arg_keys[0], (BATCH, SEQLEN, H * P_SIZE), 1.0, 6.0, ((0, 8), (1, 4))),
        "write_proj": gaussian(arg_keys[1], (BATCH, SEQLEN, G * N), 1.0, 6.0, ((0, 8), (1, 4))),
        "read_proj": gaussian(arg_keys[2], (BATCH, SEQLEN, G * N), N ** -0.5, 0.5, ((0, 8), (1, 4))),
        "dt_steps": plant(jax.random.randint(arg_keys[3], (BATCH, SEQLEN, H), 1, 17), jax.random.fold_in(arg_keys[3], 1), 1, 16).astype(jnp.int32),
        "decay_exp": draw_decay_exp(jax.random.fold_in(arg_keys[8], 71), 0),
        "norm_gain": jnp.clip(1.0 + 0.18 * jax.random.normal(arg_keys[5], (H * P_SIZE,), jnp.float32), 0.1, 1.9),
        "skip_gain": jnp.clip(1.0 + 3.0 * jax.random.uniform(arg_keys[6], (H,), jnp.float32) ** block_levels(arg_keys[6], (H,), ((0, 4),), -0.2, 0.2), 1.0, 4.0),
        "out_grad": draw_out_grad(jax.random.fold_in(arg_keys[8], 71), 0),
    }


def contract(form, left, right):
    return jnp.einsum(form, left.astype(jnp.float32), right.astype(jnp.float32))

def block_front(mixed, write, read, steps, decay):
    length = mixed.shape[0]
    log_decay = -(jnp.cumsum(jnp.transpose(decay).reshape(G, HG, length), axis=2).astype(jnp.float32) / 65536.0)
    step_size = jnp.transpose(steps).reshape(G, HG, length).astype(jnp.float32) / 16.0
    causal = jnp.arange(length)[:, None] >= jnp.arange(length)[None, :]
    spread = jnp.where(causal, log_decay[:, :, :, None] - log_decay[:, :, None, :], 0.0)
    weights = jnp.where(causal, jnp.exp(spread), 0.0) * step_size[:, :, None, :]
    scores = contract('tgn,sgn->gts', read, write)
    mixing = (scores[:, None] * weights).astype(jnp.bfloat16)
    inner_part = contract('gjts,sgjp->tgjp', mixing, mixed)
    ending = jnp.transpose(jnp.exp(log_decay[:, :, -1:] - log_decay) * step_size, (2, 0, 1))
    weighted = (mixed.astype(jnp.float32) * ending[..., None]).astype(jnp.bfloat16)
    span_state = contract('sgjp,sgn->gjpn', weighted, write).astype(jnp.bfloat16)
    block_decay = jnp.exp(log_decay[:, :, -1]).astype(jnp.bfloat16)
    readout = jnp.transpose(jnp.exp(log_decay), (2, 0, 1))
    return (weights, mixing, inner_part, ending, weighted, span_state, block_decay, readout)

def block_middle(mixed, read, skip_full, gain_full, upstream, inner_part, readout, carried):
    mixed_wide = mixed.astype(jnp.float32)
    mixer_out = inner_part + readout[..., None] * contract('tgn,gjpn->tgjp', read, carried) + skip_full[None, :, :, None] * mixed_wide
    inverse = lax.rsqrt(lax.optimization_barrier(jnp.mean(mixer_out * mixer_out, axis=(2, 3), keepdims=True)) + 1e-05)
    normed = mixer_out * inverse
    upstream_wide = upstream.astype(jnp.float32)
    normed_grad = upstream_wide * gain_full[None]
    gain_part = lax.optimization_barrier(jnp.sum(upstream_wide * normed, axis=0))
    delta_wide = inverse * (normed_grad - normed * lax.optimization_barrier(jnp.mean(normed_grad * normed, axis=(2, 3), keepdims=True)))
    skip_part = lax.optimization_barrier(jnp.sum(delta_wide * mixed_wide, axis=(0, 3)))
    delta_half = delta_wide.astype(jnp.bfloat16)
    scaled_delta = (delta_wide * readout[..., None]).astype(jnp.bfloat16)
    state_grad = contract('tgjp,tgn->gjpn', scaled_delta, read).astype(jnp.bfloat16)
    read_part = contract('tgjp,gjpn->tgn', scaled_delta, carried)
    return (delta_wide, delta_half, state_grad, read_part, gain_part, skip_part)

def block_back(mixed, write, skip_full, weights, mixing, ending, delta_wide, delta_half, read_part, carried_grad):
    mix_grad = contract('tgjp,sgjp->gjts', delta_half, mixed)
    score_grad = lax.optimization_barrier(jnp.sum(mix_grad * weights, axis=1)).astype(jnp.bfloat16)
    read_grad = contract('gts,sgn->tgn', score_grad, write) + read_part
    mixer_grad = contract('gjts,tgjp->sgjp', mixing, delta_half)
    mixer_grad = mixer_grad + ending[..., None] * contract('sgn,gjpn->sgjp', write, carried_grad)
    mixer_grad = mixer_grad + skip_full[None, :, :, None] * delta_wide
    return (mixer_grad.astype(jnp.bfloat16), read_grad.astype(jnp.bfloat16))

def forward_step(carry, item):
    decay_now, state_now = item
    updated = (decay_now.astype(jnp.float32)[..., None, None] * carry.astype(jnp.float32) + state_now.astype(jnp.float32)).astype(jnp.bfloat16)
    return (updated, carry)

def backward_step(carry, item):
    decay_now, grad_now = item
    updated = (grad_now.astype(jnp.float32) + decay_now.astype(jnp.float32)[..., None, None] * carry.astype(jnp.float32)).astype(jnp.bfloat16)
    return (updated, carry)

def one_sequence(pieces, gain_full, skip_full):
    mixed, write, read, steps, decay, upstream = pieces
    blocks = N_SEQ
    mixed = mixed.reshape(blocks, L_DEV, G, HG, P_SIZE)
    upstream = upstream.reshape(blocks, L_DEV, G, HG, P_SIZE)
    write = write.reshape(blocks, L_DEV, G, N)
    read = read.reshape(blocks, L_DEV, G, N)
    steps = steps.reshape(blocks, L_DEV, H)
    decay = decay.reshape(blocks, L_DEV, H)
    weights, mixing, inner_part, ending, weighted, span_state, block_decay, readout = jax.vmap(block_front)(mixed, write, read, steps, decay)
    start = jnp.zeros((G, HG, P_SIZE, N), jnp.bfloat16)
    final_state, carried = lax.scan(forward_step, start, (block_decay, span_state))
    middle = jax.vmap(block_middle, in_axes=(0, 0, None, None, 0, 0, 0, 0))(mixed, read, skip_full, gain_full, upstream, inner_part, readout, carried)
    delta_wide, delta_half, state_grad, read_part, gain_part, skip_part = middle
    first_grad, carried_grad = lax.scan(backward_step, start, (block_decay, state_grad), reverse=True)
    mixer_grad, read_grad = jax.vmap(block_back, in_axes=(0, 0, None, 0, 0, 0, 0, 0, 0, 0))(mixed, write, skip_full, weights, mixing, ending, delta_wide, delta_half, read_part, carried_grad)
    return (mixer_grad.reshape(SEQLEN, H * P_SIZE), read_grad.reshape(SEQLEN, G * N), lax.optimization_barrier(jnp.sum(gain_part, axis=0)), lax.optimization_barrier(jnp.sum(skip_part, axis=0)))

def reference(mixer_in, write_proj, read_proj, dt_steps, decay_exp, norm_gain, skip_gain, out_grad):
    gain_full = norm_gain.reshape(G, HG, P_SIZE)
    skip_full = skip_gain.reshape(G, HG)
    runner = partial(one_sequence, gain_full=gain_full, skip_full=skip_full)
    mixer_grad, read_grad, gain_parts, skip_parts = lax.map(runner, (mixer_in, write_proj, read_proj, dt_steps, decay_exp, out_grad))
    return (mixer_grad, read_grad, lax.optimization_barrier(jnp.sum(gain_parts, axis=0)).reshape(H * P_SIZE), lax.optimization_barrier(jnp.sum(skip_parts, axis=0)).reshape(H))
```

```python
import functools

import jax
import jax.numpy as jnp
from jax import lax
from jax.experimental import pallas as pl
from jax.experimental.pallas import tpu as pltpu
from jax.sharding import PartitionSpec as P

MESH = pl.DeviceIdType.MESH
F32, BF16 = jnp.float32, jnp.bfloat16

H = 64
P_SIZE = 64
N = 128
G = 4
HG = 16


def entering(array, axis, combine, identity, reverse):
    devices, here = (lax.axis_size(axis), lax.axis_index(axis))
    everything = jax.tree.map(lambda part: lax.all_gather(part, axis), array)
    start = jax.tree.map(
        lambda part, zero: jnp.broadcast_to(jnp.asarray(zero, part.dtype), part.shape),
        array,
        identity,
    )

    def lap(k, before):
        at = devices - 1 - k if reverse else k
        reached = at > here if reverse else at < here
        new = combine(before, jax.tree.map(lambda part: part[at], everything))
        return jax.tree.map(lambda a, b: jnp.where(reached, a, b), new, before)

    return lax.fori_loop(0, devices, lap, start)


def contract(form, left, right):
    return jnp.einsum(form, left, right, preferred_element_type=jnp.float32)


def decay_weights(log_decay, step_size):
    length = log_decay.shape[2]
    causal = jnp.arange(length)[:, None] >= jnp.arange(length)[None, :]
    spread = jnp.where(causal, log_decay[:, :, :, None] - log_decay[:, :, None, :], 0.0)
    return jnp.where(causal, jnp.exp(spread), 0.0) * step_size[:, :, None, :]


def block_front(mixed, write, read, steps, decay):
    length = mixed.shape[3]
    exponents = jnp.transpose(decay).reshape(G, HG, 1, length)
    upto = jnp.arange(length)[:, None] >= jnp.arange(length)[None, :]
    log_decay = -(jnp.sum(jnp.where(upto, exponents, 0), axis=3).astype(jnp.float32) / 65536.0)
    step_size = jnp.transpose(steps).reshape(G, HG, length).astype(jnp.float32) / 16.0
    weights = decay_weights(log_decay, step_size)
    scores = contract("gnt,gns->gts", read, write)
    mixing = (scores[:, None] * weights).astype(jnp.bfloat16)
    inner_part = contract("gjts,gjps->gjpt", mixing, mixed)
    ending = jnp.exp(log_decay[:, :, -1:] - log_decay) * step_size
    weighted = (mixed.astype(jnp.float32) * ending[:, :, None, :]).astype(jnp.bfloat16)
    span_state = contract("gjps,gns->gjpn", weighted, write).astype(jnp.bfloat16)
    block_decay = jnp.exp(log_decay[:, :, -1]).astype(jnp.bfloat16)
    readout = jnp.exp(log_decay)
    return (log_decay, step_size, mixing, inner_part, ending, span_state, block_decay, readout)


def block_middle(mixed, read, skip_full, gain_full, upstream, inner_part, readout, carried):
    mixed_wide = mixed.astype(jnp.float32)
    mixer_out = (
        inner_part
        + readout[:, :, None, :] * contract("gnt,gjpn->gjpt", read, carried)
        + skip_full[:, :, None, None] * mixed_wide
    )
    inverse = lax.rsqrt(jnp.mean(mixer_out * mixer_out, axis=(1, 2), keepdims=True) + 1e-05)
    normed = mixer_out * inverse
    upstream_wide = upstream.astype(jnp.float32)
    normed_grad = upstream_wide * gain_full[:, :, :, None]
    gain_part = jnp.sum(upstream_wide * normed, axis=3)
    delta_wide = inverse * (
        normed_grad - normed * jnp.mean(normed_grad * normed, axis=(1, 2), keepdims=True)
    )
    skip_part = jnp.sum(delta_wide * mixed_wide, axis=(2, 3))
    delta_half = delta_wide.astype(jnp.bfloat16)
    scaled_delta = (delta_wide * readout[:, :, None, :]).astype(jnp.bfloat16)
    state_grad = contract("gjpt,gnt->gjpn", scaled_delta, read).astype(jnp.bfloat16)
    read_part = contract("gjpt,gjpn->gnt", scaled_delta, carried)
    return (delta_wide, delta_half, state_grad, read_part, gain_part, skip_part)


def block_back(
    mixed,
    write,
    skip_full,
    log_decay,
    step_size,
    mixing,
    ending,
    delta_wide,
    delta_half,
    read_part,
    carried_grad,
):
    weights = decay_weights(log_decay, step_size)
    mix_grad = contract("gjpt,gjps->gjts", delta_half, mixed)
    score_grad = jnp.sum(mix_grad * weights, axis=1).astype(jnp.bfloat16)
    read_grad = contract("gts,gns->gnt", score_grad, write) + read_part
    mixer_grad = contract("gjts,gjpt->gjps", mixing, delta_half)
    mixer_grad = mixer_grad + ending[:, :, None, :] * contract(
        "gns,gjpn->gjps", write, carried_grad
    )
    mixer_grad = mixer_grad + skip_full[:, :, None, None] * delta_wide
    return (mixer_grad.astype(jnp.bfloat16), read_grad.astype(jnp.bfloat16))


def forward_join(earlier, later):
    decay_early, state_early = earlier
    decay_late, state_late = later
    joined = (decay_early.astype(jnp.float32) * decay_late.astype(jnp.float32)).astype(jnp.bfloat16)
    state = (
        decay_late.astype(jnp.float32)[..., None, None] * state_early.astype(jnp.float32)
        + state_late.astype(jnp.float32)
    ).astype(jnp.bfloat16)
    return (joined, state)


def backward_join(earlier, later):
    decay_early, grad_early = earlier
    decay_late, grad_late = later
    joined = (decay_early.astype(jnp.float32) * decay_late.astype(jnp.float32)).astype(jnp.bfloat16)
    grads = (
        grad_late.astype(jnp.float32)
        + decay_late.astype(jnp.float32)[..., None, None] * grad_early.astype(jnp.float32)
    ).astype(jnp.bfloat16)
    return (joined, grads)


def neutral(block_decay, span_state):
    return (jnp.ones(block_decay.shape, jnp.bfloat16), jnp.zeros(span_state.shape, jnp.bfloat16))


def states_whole(block_decay, span_state):
    return entering(
        (block_decay, span_state), "seq", forward_join, neutral(block_decay, span_state), False
    )[1]


def grads_whole(block_decay, state_grad):
    return entering(
        (block_decay, state_grad), "seq", backward_join, neutral(block_decay, state_grad), True
    )[1]


def on_device(mixer_in, write_proj, read_proj, dt_steps, decay_exp, norm_gain, skip_gain, out_grad):
    length = mixer_in.shape[1]
    mixed = jnp.transpose(mixer_in[0].reshape(length, G, HG, P_SIZE), (1, 2, 3, 0))
    upstream = jnp.transpose(out_grad[0].reshape(length, G, HG, P_SIZE), (1, 2, 3, 0))
    write = jnp.transpose(write_proj[0].reshape(length, G, N), (1, 2, 0))
    read = jnp.transpose(read_proj[0].reshape(length, G, N), (1, 2, 0))
    gain_whole, skip_whole = (
        lax.all_gather(norm_gain, "seq", axis=0, tiled=True),
        lax.all_gather(skip_gain, "seq", axis=0, tiled=True),
    )
    gain_full = gain_whole.reshape(G, HG, P_SIZE)
    skip_full = skip_whole.reshape(G, HG)
    log_decay, step_size, mixing, inner_part, ending, span_state, block_decay, readout = (
        block_front(mixed, write, read, dt_steps[0], decay_exp[0])
    )
    carried = states_whole(block_decay, span_state)
    delta_wide, delta_half, state_grad, read_part, gain_part, skip_part = block_middle(
        mixed, read, skip_full, gain_full, upstream, inner_part, readout, carried
    )
    carried_grad = grads_whole(block_decay, state_grad)
    mixer_grad, read_grad = block_back(
        mixed,
        write,
        skip_full,
        log_decay,
        step_size,
        mixing,
        ending,
        delta_wide,
        delta_half,
        read_part,
        carried_grad,
    )
    gain_flat = gain_part.reshape(H * P_SIZE)
    skip_flat = skip_part.reshape(H)
    gain_share, skip_share = (
        lax.psum_scatter(gain_flat, "seq", scatter_dimension=0, tiled=True),
        lax.psum_scatter(skip_flat, "seq", scatter_dimension=0, tiled=True),
    )
    gain_piece, skip_piece = lax.psum((gain_share, skip_share), "rep")
    mixer_rows = jnp.transpose(mixer_grad, (3, 0, 1, 2)).reshape(1, length, H * P_SIZE)
    read_rows = jnp.transpose(read_grad, (2, 0, 1)).reshape(1, length, G * N)
    return (mixer_rows, read_rows, gain_piece, skip_piece)


def mm(a, b, dims):
    return lax.dot_general(a, b, (dims, ((), ())), preferred_element_type=F32)


NN, NT, TN = ((1,), (0,)), ((1,), (1,)), ((0,), (0,))


def grouped_kernel(
    n,
    reps,
    x_ref,
    b_ref,
    c_ref,
    u_ref,
    steps_ref,
    decay_ref,
    gain_ref,
    skip_ref,
    out_ref,
    read_ref,
    sums_ref,
    xs,
    us,
    bs,
    cs,
    table_out,
    table,
    cols,
    ends,
    mix,
    weights,
    y,
    half,
    inv,
    carried,
    carried_grad,
    read_part,
    grad_out,
    read_out,
    sums,
    send_sem,
    recv_sem,
    local_sem,
    rep_send,
    rep_recv,
):
    me, my_rep = lax.axis_index("seq"), lax.axis_index("rep")
    length, width, state = xs.shape[1], xs.shape[2], bs.shape[2]
    heads = table.shape[1] // 2
    pairs = width // (2 * P_SIZE)
    lanes = 2 * P_SIZE
    peers = [lax.rem(me + d, n) for d in range(1, n)]
    rep_peers = [lax.rem(my_rep + d, reps) for d in range(1, reps)]

    barrier = pltpu.get_barrier_semaphore()
    for peer in peers:
        pl.semaphore_signal(barrier, inc=1, device_id={"seq": peer}, device_id_type=MESH)
    for peer in rep_peers:
        pl.semaphore_signal(barrier, inc=1, device_id={"rep": peer}, device_id_type=MESH)

    row = lax.broadcasted_iota(jnp.int32, (length, length), 0)
    col = lax.broadcasted_iota(jnp.int32, (length, length), 1)
    causal = row >= col
    left = lax.broadcasted_iota(jnp.int32, (length, lanes), 1) < P_SIZE
    left_row = lax.broadcasted_iota(jnp.int32, (1, lanes), 1) < P_SIZE

    triangle = jnp.where(causal, 1.0, 0.0).astype(BF16)
    decay = decay_ref[...]
    high = (decay >> 8).astype(F32).astype(BF16)
    low = (decay & 255).astype(F32).astype(BF16)
    total = mm(triangle, high, NN) * 256.0 + mm(triangle, low, NN)
    both = jnp.concatenate([total * (-1.0 / 65536.0), steps_ref[...].astype(F32) / 16.0], axis=1)
    flipped = both.T
    for g in range(n):
        table_out[g, :heads] = flipped[g * heads : (g + 1) * heads]
        table_out[g, heads:] = flipped[(n + g) * heads : (n + g + 1) * heads]

    def part(ref, g, size):
        return ref.at[:, pl.ds(pl.multiple_of(g * size, size), size)]

    def source(a, g):
        if a == 0:
            return table_out.at[g]
        return part((x_ref, b_ref, c_ref, u_ref)[a - 1], g, (width, state, state, width)[a - 1])

    target = (table, xs, bs, cs, us)

    def send(a, d):
        return pltpu.make_async_remote_copy(
            src_ref=source(a, peers[d]),
            dst_ref=target[a].at[me],
            send_sem=send_sem.at[a, d],
            recv_sem=recv_sem.at[a, me],
            device_id={"seq": peers[d]},
            device_id_type=MESH,
        )

    def arrival(a, d):
        return pltpu.make_async_remote_copy(
            src_ref=source(a, peers[d]),
            dst_ref=target[a].at[peers[d]],
            send_sem=send_sem.at[a, d],
            recv_sem=recv_sem.at[a, peers[d]],
            device_id={"seq": peers[d]},
            device_id_type=MESH,
        )

    own = [
        pltpu.make_async_copy(source(a, me), target[a].at[me], local_sem.at[a]) for a in range(5)
    ]
    for copy in own:
        copy.start()
    pl.semaphore_wait(barrier, n - 1 + reps - 1)
    for a in range(4):
        for d in range(n - 1):
            send(a, d).start()
    for copy in own:
        copy.wait()
    for a in range(4):
        for d in range(n - 1):
            arrival(a, d).wait_recv()
    for d in range(n - 1):
        send(4, d).start()

    def span(j):
        return slice(j * lanes, (j + 1) * lanes)

    def pick(values, j):
        return jnp.where(left, values[:, 2 * j : 2 * j + 1], values[:, 2 * j + 1 : 2 * j + 2])

    def pick_row(values, j):
        return jnp.where(left_row, values[:, 2 * j : 2 * j + 1], values[:, 2 * j + 1 : 2 * j + 2])

    def skip_pair(j):
        return jnp.where(left_row, skip_ref[2 * j], skip_ref[2 * j + 1])

    def apart(values):
        zero = jnp.zeros_like(values)
        return jnp.concatenate([jnp.where(left, values, zero), jnp.where(left, zero, values)], axis=0)

    def closing(k):
        return jnp.exp(cols[k][length - 1 :, :]).astype(BF16).astype(F32)

    carried[0] = jnp.zeros(carried.shape[1:], BF16)
    carried_grad[n] = jnp.zeros(carried_grad.shape[1:], BF16)

    def forward(k, _):
        tab = table[k]
        copies = length // (2 * heads)
        c = jnp.concatenate([tab] * copies, axis=0).T
        swapped = jnp.concatenate([tab[heads:], tab[:heads]] * copies, axis=0).T
        cols[k] = c
        ending = jnp.exp(c[length - 1 :, :] - c) * swapped
        ends[k] = ending
        readout = jnp.exp(c)
        block_decay = closing(k)
        write, read = bs[k], cs[k]
        scores = mm(read, write, NT)
        squares = jnp.zeros((length, lanes), F32)
        for j in range(pairs):
            mixed = []
            for e in range(2):
                h = 2 * j + e
                spread = jnp.where(causal, c[:, h : h + 1] - tab[h : h + 1, :], -1e30)
                w = jnp.exp(spread) * tab[heads + h : heads + h + 1, :]
                weights[k, j, :, e * length : (e + 1) * length] = w
                mixed.append((scores * w).astype(BF16))
            mixing = jnp.concatenate(mixed, axis=1)
            mix[k, j] = mixing
            x = xs[k, :, span(j)]
            wide = x.astype(F32)
            before = carried[k, :, span(j)]
            out = mm(mixing, apart(x), NN)
            out = out + pick(readout, j) * mm(read, before, NN) + skip_pair(j) * wide
            y[k, :, span(j)] = out
            squares = squares + out * out
            weighted = (wide * pick(ending, j)).astype(BF16)
            grown = mm(write, weighted, TN).astype(BF16).astype(F32)
            carried[k + 1, :, span(j)] = (
                pick_row(block_decay, j) * before.astype(F32) + grown
            ).astype(BF16)
        mean = jnp.sum(squares, axis=1, keepdims=True) / width
        inv[k] = jnp.broadcast_to(lax.rsqrt(mean + 1e-05), inv.shape[1:])
        return 0

    lax.fori_loop(0, n, forward, 0)

    for d in range(n - 1):
        arrival(4, d).wait_recv()
    sums[my_rep] = jnp.zeros(sums.shape[1:], F32)

    def middle(i, _):
        k = n - 1 - i
        inverse = inv[k]
        readout = jnp.exp(cols[k])
        block_decay = closing(k)
        read = cs[k]
        inner = jnp.zeros((length, lanes), F32)
        for j in range(pairs):
            up = us[k, :, span(j)].astype(F32)
            normed = y[k, :, span(j)] * inverse
            product = up * normed
            inner = inner + product * gain_ref[:, span(j)]
            sums[my_rep, 0:1, span(j)] += jnp.sum(product, axis=0, keepdims=True)
        mean = jnp.sum(inner, axis=1, keepdims=True) / width
        kept = jnp.zeros((length, state), F32)
        for j in range(pairs):
            up = us[k, :, span(j)].astype(F32)
            normed = y[k, :, span(j)] * inverse
            delta = inverse * (up * gain_ref[:, span(j)] - normed * mean)
            y[k, :, span(j)] = delta
            half[k, :, span(j)] = delta.astype(BF16)
            wide = xs[k, :, span(j)].astype(F32)
            sums[my_rep, 1:2, span(j)] += jnp.sum(delta * wide, axis=0, keepdims=True)
            scaled = (delta * pick(readout, j)).astype(BF16)
            state_grad = mm(read, scaled, TN).astype(BF16).astype(F32)
            kept = kept + mm(scaled, carried[k, :, span(j)], NT)
            later = carried_grad[k + 1, :, span(j)].astype(F32)
            carried_grad[k, :, span(j)] = (
                state_grad + pick_row(block_decay, j) * later
            ).astype(BF16)
        read_part[k] = kept
        return 0

    lax.fori_loop(0, n, middle, 0)

    def rep_send_copy(d):
        return pltpu.make_async_remote_copy(
            src_ref=sums.at[my_rep],
            dst_ref=sums.at[my_rep],
            send_sem=rep_send.at[d],
            recv_sem=rep_recv.at[my_rep],
            device_id={"rep": rep_peers[d]},
            device_id_type=MESH,
        )

    def rep_arrival(d):
        return pltpu.make_async_remote_copy(
            src_ref=sums.at[my_rep],
            dst_ref=sums.at[rep_peers[d]],
            send_sem=rep_send.at[d],
            recv_sem=rep_recv.at[rep_peers[d]],
            device_id={"rep": rep_peers[d]},
            device_id_type=MESH,
        )

    for d in range(reps - 1):
        rep_send_copy(d).start()

    def results(d, k):
        return [
            pltpu.make_async_remote_copy(
                src_ref=values.at[k],
                dst_ref=part(ref, me, size),
                send_sem=send_sem.at[a, d],
                recv_sem=recv_sem.at[a, me],
                device_id={"seq": k},
                device_id_type=MESH,
            )
            for a, values, ref, size in (
                (5, grad_out, out_ref, width),
                (6, read_out, read_ref, state),
            )
        ]

    def result_arrivals(d):
        peer = peers[d]
        return [
            pltpu.make_async_remote_copy(
                src_ref=values.at[peer],
                dst_ref=part(ref, peer, size),
                send_sem=send_sem.at[a, d],
                recv_sem=recv_sem.at[a, peer],
                device_id={"seq": peer},
                device_id_type=MESH,
            )
            for a, values, ref, size in (
                (5, grad_out, out_ref, width),
                (6, read_out, read_ref, state),
            )
        ]

    def back(i, _):
        k = lax.rem(me + 1 + i, n)
        write = bs[k]
        ending = ends[k]
        grads = jnp.zeros((length, length), F32)
        for j in range(pairs):
            delta = half[k, :, span(j)]
            product = mm(delta, apart(xs[k, :, span(j)]), NT) * weights[k, j]
            grads = grads + product[:, :length] + product[:, length:]
            turned = mm(mix[k, j], delta, TN)
            out = jnp.where(left, turned[:length], turned[length:])
            out = out + pick(ending, j) * mm(write, carried_grad[k + 1, :, span(j)], NN)
            out = out + skip_pair(j) * y[k, :, span(j)]
            grad_out[k, :, span(j)] = out.astype(BF16)
        read_out[k] = (mm(grads.astype(BF16), write, NN) + read_part[k]).astype(BF16)

        @pl.when(i < n - 1)
        def _():
            for copy in results(i, k):
                copy.start()

        return 0

    lax.fori_loop(0, n, back, 0)

    last = [
        pltpu.make_async_copy(grad_out.at[me], part(out_ref, me, width), local_sem.at[5]),
        pltpu.make_async_copy(read_out.at[me], part(read_ref, me, state), local_sem.at[6]),
    ]
    for copy in last:
        copy.start()
    for d in range(reps - 1):
        rep_arrival(d).wait_recv()
    everything = sums[0]
    for r in range(1, reps):
        everything = everything + sums[r]
    sums_ref[...] = everything
    for d in range(n - 1):
        for a in range(5):
            send(a, d).wait_send()
        for copy in results(d, peers[d]):
            copy.wait_send()
        for copy in result_arrivals(d):
            copy.wait_recv()
    for d in range(reps - 1):
        rep_send_copy(d).wait_send()
    for copy in last:
        copy.wait()


def by_groups(n, reps, mixer_in, write_proj, read_proj, dt_steps, decay_exp, norm_gain, skip_gain, out_grad):
    length, channels = mixer_in.shape[1:]
    width, state = channels // n, write_proj.shape[2] // n
    heads = width // P_SIZE
    pairs = heads // 2
    hbm = pl.BlockSpec(memory_space=pl.ANY)
    vmem = pl.BlockSpec(memory_space=pltpu.VMEM)
    smem = pl.BlockSpec(memory_space=pltpu.SMEM)
    wide, square = (n, length, width), (n, length, state)
    mixer_grad, read_grad, sums = pl.pallas_call(
        functools.partial(grouped_kernel, n, reps),
        out_shape=(
            jax.ShapeDtypeStruct((length, channels), BF16),
            jax.ShapeDtypeStruct((length, n * state), BF16),
            jax.ShapeDtypeStruct((2, width), F32),
        ),
        in_specs=[hbm, hbm, hbm, hbm, vmem, vmem, vmem, smem],
        out_specs=(hbm, hbm, vmem),
        scratch_shapes=[
            pltpu.VMEM(wide, BF16),
            pltpu.VMEM(wide, BF16),
            pltpu.VMEM(square, BF16),
            pltpu.VMEM(square, BF16),
            pltpu.VMEM((n, 2 * heads, length), F32),
            pltpu.VMEM((n, 2 * heads, length), F32),
            pltpu.VMEM((n, length, length), F32),
            pltpu.VMEM((n, length, length), F32),
            pltpu.VMEM((n, pairs, length, 2 * length), BF16),
            pltpu.VMEM((n, pairs, length, 2 * length), F32),
            pltpu.VMEM(wide, F32),
            pltpu.VMEM(wide, BF16),
            pltpu.VMEM((n, length, 2 * P_SIZE), F32),
            pltpu.VMEM((n + 1, state, width), BF16),
            pltpu.VMEM((n + 1, state, width), BF16),
            pltpu.VMEM(square, F32),
            pltpu.VMEM(wide, BF16),
            pltpu.VMEM(square, BF16),
            pltpu.VMEM((reps, 2, width), F32),
            pltpu.SemaphoreType.DMA((7, n - 1)),
            pltpu.SemaphoreType.DMA((7, n)),
            pltpu.SemaphoreType.DMA((7,)),
            pltpu.SemaphoreType.DMA((max(reps - 1, 1),)),
            pltpu.SemaphoreType.DMA((reps,)),
        ],
        compiler_params=pltpu.CompilerParams(
            collective_id=0, has_side_effects=True, vmem_limit_bytes=48 * 1024 * 1024
        ),
    )(
        mixer_in[0],
        write_proj[0],
        read_proj[0],
        out_grad[0],
        dt_steps[0],
        decay_exp[0],
        norm_gain.reshape(1, width),
        skip_gain,
    )
    skip_grad = jnp.sum(sums[1].reshape(heads, P_SIZE), axis=1)
    return (mixer_grad[None], read_grad[None], sums[0], skip_grad)


def solution(mesh):
    n, reps = mesh.shape["seq"], mesh.shape["rep"]

    def step(*args):
        batch, length = args[0].shape[:2]
        if n == G and batch == 1 and length == N and 2 * P_SIZE == N:
            return by_groups(n, reps, *args)
        return on_device(*args)

    in_specs = (
        P("rep", "seq", None),
        P("rep", "seq", None),
        P("rep", "seq", None),
        P("rep", "seq", None),
        P("rep", "seq", None),
        P("seq"),
        P("seq"),
        P("rep", "seq", None),
    )
    out_specs = (P("rep", "seq", None), P("rep", "seq", None), P("seq"), P("seq"))
    return jax.shard_map(
        step, mesh=mesh, in_specs=in_specs, out_specs=out_specs, check_vma=False
    )
```

```python
import functools

import jax
import jax.numpy as jnp
from jax import lax
from jax.experimental import pallas as pl
from jax.experimental.pallas import tpu as pltpu
from jax.sharding import PartitionSpec as P

MESH = pl.DeviceIdType.MESH
F32, BF16 = jnp.float32, jnp.bfloat16

H = 64
P_SIZE = 64
N = 128
G = 4
HG = 16


def entering(array, axis, combine, identity, reverse):
    devices, here = (lax.axis_size(axis), lax.axis_index(axis))
    everything = jax.tree.map(lambda part: lax.all_gather(part, axis), array)
    start = jax.tree.map(
        lambda part, zero: jnp.broadcast_to(jnp.asarray(zero, part.dtype), part.shape),
        array,
        identity,
    )

    def lap(k, before):
        at = devices - 1 - k if reverse else k
        reached = at > here if reverse else at < here
        new = combine(before, jax.tree.map(lambda part: part[at], everything))
        return jax.tree.map(lambda a, b: jnp.where(reached, a, b), new, before)

    return lax.fori_loop(0, devices, lap, start)


def contract(form, left, right):
    return jnp.einsum(form, left, right, preferred_element_type=jnp.float32)


def decay_weights(log_decay, step_size):
    length = log_decay.shape[2]
    causal = jnp.arange(length)[:, None] >= jnp.arange(length)[None, :]
    spread = jnp.where(causal, log_decay[:, :, :, None] - log_decay[:, :, None, :], 0.0)
    return jnp.where(causal, jnp.exp(spread), 0.0) * step_size[:, :, None, :]


def block_front(mixed, write, read, steps, decay):
    length = mixed.shape[3]
    exponents = jnp.transpose(decay).reshape(G, HG, 1, length)
    upto = jnp.arange(length)[:, None] >= jnp.arange(length)[None, :]
    log_decay = -(jnp.sum(jnp.where(upto, exponents, 0), axis=3).astype(jnp.float32) / 65536.0)
    step_size = jnp.transpose(steps).reshape(G, HG, length).astype(jnp.float32) / 16.0
    weights = decay_weights(log_decay, step_size)
    scores = contract("gnt,gns->gts", read, write)
    mixing = (scores[:, None] * weights).astype(jnp.bfloat16)
    inner_part = contract("gjts,gjps->gjpt", mixing, mixed)
    ending = jnp.exp(log_decay[:, :, -1:] - log_decay) * step_size
    weighted = (mixed.astype(jnp.float32) * ending[:, :, None, :]).astype(jnp.bfloat16)
    span_state = contract("gjps,gns->gjpn", weighted, write).astype(jnp.bfloat16)
    block_decay = jnp.exp(log_decay[:, :, -1]).astype(jnp.bfloat16)
    readout = jnp.exp(log_decay)
    return (log_decay, step_size, mixing, inner_part, ending, span_state, block_decay, readout)


def block_middle(mixed, read, skip_full, gain_full, upstream, inner_part, readout, carried):
    mixed_wide = mixed.astype(jnp.float32)
    mixer_out = (
        inner_part
        + readout[:, :, None, :] * contract("gnt,gjpn->gjpt", read, carried)
        + skip_full[:, :, None, None] * mixed_wide
    )
    inverse = lax.rsqrt(jnp.mean(mixer_out * mixer_out, axis=(1, 2), keepdims=True) + 1e-05)
    normed = mixer_out * inverse
    upstream_wide = upstream.astype(jnp.float32)
    normed_grad = upstream_wide * gain_full[:, :, :, None]
    gain_part = jnp.sum(upstream_wide * normed, axis=3)
    delta_wide = inverse * (
        normed_grad - normed * jnp.mean(normed_grad * normed, axis=(1, 2), keepdims=True)
    )
    skip_part = jnp.sum(delta_wide * mixed_wide, axis=(2, 3))
    delta_half = delta_wide.astype(jnp.bfloat16)
    scaled_delta = (delta_wide * readout[:, :, None, :]).astype(jnp.bfloat16)
    state_grad = contract("gjpt,gnt->gjpn", scaled_delta, read).astype(jnp.bfloat16)
    read_part = contract("gjpt,gjpn->gnt", scaled_delta, carried)
    return (delta_wide, delta_half, state_grad, read_part, gain_part, skip_part)


def block_back(
    mixed,
    write,
    skip_full,
    log_decay,
    step_size,
    mixing,
    ending,
    delta_wide,
    delta_half,
    read_part,
    carried_grad,
):
    weights = decay_weights(log_decay, step_size)
    mix_grad = contract("gjpt,gjps->gjts", delta_half, mixed)
    score_grad = jnp.sum(mix_grad * weights, axis=1).astype(jnp.bfloat16)
    read_grad = contract("gts,gns->gnt", score_grad, write) + read_part
    mixer_grad = contract("gjts,gjpt->gjps", mixing, delta_half)
    mixer_grad = mixer_grad + ending[:, :, None, :] * contract(
        "gns,gjpn->gjps", write, carried_grad
    )
    mixer_grad = mixer_grad + skip_full[:, :, None, None] * delta_wide
    return (mixer_grad.astype(jnp.bfloat16), read_grad.astype(jnp.bfloat16))


def forward_join(earlier, later):
    decay_early, state_early = earlier
    decay_late, state_late = later
    joined = (decay_early.astype(jnp.float32) * decay_late.astype(jnp.float32)).astype(jnp.bfloat16)
    state = (
        decay_late.astype(jnp.float32)[..., None, None] * state_early.astype(jnp.float32)
        + state_late.astype(jnp.float32)
    ).astype(jnp.bfloat16)
    return (joined, state)


def backward_join(earlier, later):
    decay_early, grad_early = earlier
    decay_late, grad_late = later
    joined = (decay_early.astype(jnp.float32) * decay_late.astype(jnp.float32)).astype(jnp.bfloat16)
    grads = (
        grad_late.astype(jnp.float32)
        + decay_late.astype(jnp.float32)[..., None, None] * grad_early.astype(jnp.float32)
    ).astype(jnp.bfloat16)
    return (joined, grads)


def neutral(block_decay, span_state):
    return (jnp.ones(block_decay.shape, jnp.bfloat16), jnp.zeros(span_state.shape, jnp.bfloat16))


def states_whole(block_decay, span_state):
    return entering(
        (block_decay, span_state), "seq", forward_join, neutral(block_decay, span_state), False
    )[1]


def grads_whole(block_decay, state_grad):
    return entering(
        (block_decay, state_grad), "seq", backward_join, neutral(block_decay, state_grad), True
    )[1]


def on_device(mixer_in, write_proj, read_proj, dt_steps, decay_exp, norm_gain, skip_gain, out_grad):
    length = mixer_in.shape[1]
    mixed = jnp.transpose(mixer_in[0].reshape(length, G, HG, P_SIZE), (1, 2, 3, 0))
    upstream = jnp.transpose(out_grad[0].reshape(length, G, HG, P_SIZE), (1, 2, 3, 0))
    write = jnp.transpose(write_proj[0].reshape(length, G, N), (1, 2, 0))
    read = jnp.transpose(read_proj[0].reshape(length, G, N), (1, 2, 0))
    gain_whole, skip_whole = (
        lax.all_gather(norm_gain, "seq", axis=0, tiled=True),
        lax.all_gather(skip_gain, "seq", axis=0, tiled=True),
    )
    gain_full = gain_whole.reshape(G, HG, P_SIZE)
    skip_full = skip_whole.reshape(G, HG)
    log_decay, step_size, mixing, inner_part, ending, span_state, block_decay, readout = (
        block_front(mixed, write, read, dt_steps[0], decay_exp[0])
    )
    carried = states_whole(block_decay, span_state)
    delta_wide, delta_half, state_grad, read_part, gain_part, skip_part = block_middle(
        mixed, read, skip_full, gain_full, upstream, inner_part, readout, carried
    )
    carried_grad = grads_whole(block_decay, state_grad)
    mixer_grad, read_grad = block_back(
        mixed,
        write,
        skip_full,
        log_decay,
        step_size,
        mixing,
        ending,
        delta_wide,
        delta_half,
        read_part,
        carried_grad,
    )
    gain_flat = gain_part.reshape(H * P_SIZE)
    skip_flat = skip_part.reshape(H)
    gain_share, skip_share = (
        lax.psum_scatter(gain_flat, "seq", scatter_dimension=0, tiled=True),
        lax.psum_scatter(skip_flat, "seq", scatter_dimension=0, tiled=True),
    )
    gain_piece, skip_piece = lax.psum((gain_share, skip_share), "rep")
    mixer_rows = jnp.transpose(mixer_grad, (3, 0, 1, 2)).reshape(1, length, H * P_SIZE)
    read_rows = jnp.transpose(read_grad, (2, 0, 1)).reshape(1, length, G * N)
    return (mixer_rows, read_rows, gain_piece, skip_piece)


def mm(a, b, dims):
    return lax.dot_general(a, b, (dims, ((), ())), preferred_element_type=F32)


NN, NT, TN = ((1,), (0,)), ((1,), (1,)), ((0,), (0,))


def grouped_kernel(
    n,
    reps,
    x_ref,
    b_ref,
    c_ref,
    u_ref,
    steps_ref,
    decay_ref,
    gain_ref,
    skip_ref,
    out_ref,
    read_ref,
    gain_out,
    skip_out,
    xs,
    us,
    bs,
    cs,
    table_out,
    table,
    cols,
    ends,
    mix,
    weights,
    y,
    half,
    inv,
    carried,
    carried_grad,
    read_part,
    grad_out,
    read_out,
    sums,
    send_sem,
    recv_sem,
    local_sem,
    rep_send,
    rep_recv,
):
    me, my_rep = lax.axis_index("seq"), lax.axis_index("rep")
    length, width, state = xs.shape[1], xs.shape[2], bs.shape[2]
    heads = table.shape[1] // 2
    pairs = width // (2 * P_SIZE)
    lanes = 2 * P_SIZE
    swap = lax.rem(my_rep, 2)

    def partner(i):
        step = lax.rem(i + 1, n)
        minor, major = lax.rem(step, 2), step // 2
        minor, major = minor + swap * (major - minor), major + swap * (minor - major)
        return lax.rem(me + minor, 2) + 2 * lax.rem(me // 2 + major, 2)

    peers = [partner(d) for d in range(n - 1)]
    rep_peers = [lax.rem(my_rep + d, reps) for d in range(1, reps)]

    barrier = pltpu.get_barrier_semaphore()
    for peer in peers:
        pl.semaphore_signal(barrier, inc=1, device_id={"seq": peer}, device_id_type=MESH)
    for peer in rep_peers:
        pl.semaphore_signal(barrier, inc=1, device_id={"rep": peer}, device_id_type=MESH)

    row = lax.broadcasted_iota(jnp.int32, (length, length), 0)
    col = lax.broadcasted_iota(jnp.int32, (length, length), 1)
    causal = row >= col
    left = lax.broadcasted_iota(jnp.int32, (length, lanes), 1) < P_SIZE
    left_row = lax.broadcasted_iota(jnp.int32, (1, lanes), 1) < P_SIZE

    triangle = jnp.where(row <= col, 1.0, 0.0).astype(BF16)
    decay = decay_ref[...]
    high = (decay >> 8).astype(F32).astype(BF16)
    low = (decay & 255).astype(F32).astype(BF16)
    total = mm(high, triangle, NN) * 256.0 + mm(low, triangle, NN)
    log_decay, step_size = total * (-1.0 / 65536.0), steps_ref[...].astype(F32) / 16.0
    for g in range(n):
        table_out[g, :heads] = log_decay[g * heads : (g + 1) * heads]
        table_out[g, heads:] = step_size[g * heads : (g + 1) * heads]

    def part(ref, g, size):
        return ref.at[:, pl.ds(pl.multiple_of(g * size, size), size)]

    def source(a, g):
        if a == 0:
            return table_out.at[g]
        return part((x_ref, b_ref, c_ref, u_ref)[a - 1], g, (width, state, state, width)[a - 1])

    target = (table, xs, bs, cs, us)

    def send(a, d):
        return pltpu.make_async_remote_copy(
            src_ref=source(a, peers[d]),
            dst_ref=target[a].at[me],
            send_sem=send_sem.at[a, d],
            recv_sem=recv_sem.at[a, me],
            device_id={"seq": peers[d]},
            device_id_type=MESH,
        )

    def arrival(a, d):
        return pltpu.make_async_remote_copy(
            src_ref=source(a, peers[d]),
            dst_ref=target[a].at[peers[d]],
            send_sem=send_sem.at[a, d],
            recv_sem=recv_sem.at[a, peers[d]],
            device_id={"seq": peers[d]},
            device_id_type=MESH,
        )

    own = [
        pltpu.make_async_copy(source(a, me), target[a].at[me], local_sem.at[a]) for a in range(5)
    ]
    for copy in own:
        copy.start()
    pl.semaphore_wait(barrier, n - 1 + reps - 1)
    for a in (0, 2, 3, 1):
        for d in range(n - 1):
            send(a, d).start()
    for copy in own:
        copy.wait()
    for a in (0, 2, 3):
        for d in range(n - 1):
            arrival(a, d).wait_recv()

    def span(j):
        return slice(j * lanes, (j + 1) * lanes)

    def pick(values, j):
        return jnp.where(left, values[:, 2 * j : 2 * j + 1], values[:, 2 * j + 1 : 2 * j + 2])

    def pick_row(values, j):
        return jnp.where(left_row, values[:, 2 * j : 2 * j + 1], values[:, 2 * j + 1 : 2 * j + 2])

    def skip_pair(j):
        return jnp.where(left_row, skip_ref[2 * j], skip_ref[2 * j + 1])

    def apart(values):
        zero = jnp.zeros_like(values)
        return jnp.concatenate([jnp.where(left, values, zero), jnp.where(left, zero, values)], axis=0)

    def closing(k):
        return jnp.exp(cols[k][length - 1 :, :]).astype(BF16).astype(F32)

    carried[0] = jnp.zeros(carried.shape[1:], BF16)
    carried_grad[n] = jnp.zeros(carried_grad.shape[1:], BF16)

    def front(k, _):
        tab = table[k]
        copies = length // (2 * heads)
        c = jnp.concatenate([tab] * copies, axis=0).T
        swapped = jnp.concatenate([tab[heads:], tab[:heads]] * copies, axis=0).T
        cols[k] = c
        ends[k] = jnp.exp(c[length - 1 :, :] - c) * swapped
        scores = mm(cs[k], bs[k], NT)
        for j in range(pairs):
            for e in range(2):
                h = 2 * j + e
                spread = jnp.where(causal, c[:, h : h + 1] - tab[h : h + 1, :], -1e30)
                w = jnp.exp(spread) * tab[heads + h : heads + h + 1, :]
                weights[k, j, :, e * length : (e + 1) * length] = w
                mix[k, j, :, e * length : (e + 1) * length] = (scores * w).astype(BF16)
        return 0

    lax.fori_loop(0, n, front, 0)

    for d in range(n - 1):
        send(4, d).start()
    for d in range(n - 1):
        arrival(1, d).wait_recv()

    def forward(k, _):
        ending = ends[k]
        readout = jnp.exp(cols[k])
        block_decay = closing(k)
        write, read = bs[k], cs[k]
        squares = jnp.zeros((length, lanes), F32)
        for j in range(pairs):
            x = xs[k, :, span(j)]
            wide = x.astype(F32)
            before = carried[k, :, span(j)]
            out = mm(mix[k, j], apart(x), NN)
            out = out + pick(readout, j) * mm(read, before, NN) + skip_pair(j) * wide
            y[k, :, span(j)] = out
            squares = squares + out * out
            weighted = (wide * pick(ending, j)).astype(BF16)
            grown = mm(write, weighted, TN).astype(BF16).astype(F32)
            carried[k + 1, :, span(j)] = (
                pick_row(block_decay, j) * before.astype(F32) + grown
            ).astype(BF16)
        mean = jnp.sum(squares, axis=1, keepdims=True) / width
        inv[k] = jnp.broadcast_to(lax.rsqrt(mean + 1e-05), inv.shape[1:])
        return 0

    lax.fori_loop(0, n, forward, 0)

    for d in range(n - 1):
        arrival(4, d).wait_recv()
    sums[my_rep] = jnp.zeros(sums.shape[1:], F32)

    def middle(i, _):
        k = n - 1 - i
        inverse = inv[k]
        readout = jnp.exp(cols[k])
        block_decay = closing(k)
        read = cs[k]
        inner = jnp.zeros((length, lanes), F32)
        for j in range(pairs):
            up = us[k, :, span(j)].astype(F32)
            normed = y[k, :, span(j)] * inverse
            product = up * normed
            inner = inner + product * gain_ref[:, span(j)]
            sums[my_rep, 0:1, span(j)] += jnp.sum(product, axis=0, keepdims=True)
        mean = jnp.sum(inner, axis=1, keepdims=True) / width
        kept = jnp.zeros((length, state), F32)
        for j in range(pairs):
            up = us[k, :, span(j)].astype(F32)
            normed = y[k, :, span(j)] * inverse
            delta = inverse * (up * gain_ref[:, span(j)] - normed * mean)
            y[k, :, span(j)] = delta
            half[k, :, span(j)] = delta.astype(BF16)
            wide = xs[k, :, span(j)].astype(F32)
            sums[my_rep, 1:2, span(j)] += jnp.sum(delta * wide, axis=0, keepdims=True)
            scaled = (delta * pick(readout, j)).astype(BF16)
            state_grad = mm(read, scaled, TN).astype(BF16).astype(F32)
            kept = kept + mm(scaled, carried[k, :, span(j)], NT)
            later = carried_grad[k + 1, :, span(j)].astype(F32)
            carried_grad[k, :, span(j)] = (
                state_grad + pick_row(block_decay, j) * later
            ).astype(BF16)
        read_part[k] = kept
        return 0

    lax.fori_loop(0, n, middle, 0)

    def rep_send_copy(d):
        return pltpu.make_async_remote_copy(
            src_ref=sums.at[my_rep],
            dst_ref=sums.at[my_rep],
            send_sem=rep_send.at[d],
            recv_sem=rep_recv.at[my_rep],
            device_id={"rep": rep_peers[d]},
            device_id_type=MESH,
        )

    def rep_arrival(d):
        return pltpu.make_async_remote_copy(
            src_ref=sums.at[my_rep],
            dst_ref=sums.at[rep_peers[d]],
            send_sem=rep_send.at[d],
            recv_sem=rep_recv.at[rep_peers[d]],
            device_id={"rep": rep_peers[d]},
            device_id_type=MESH,
        )

    for d in range(reps - 1):
        rep_send_copy(d).start()

    def results(d, k):
        return [
            pltpu.make_async_remote_copy(
                src_ref=values.at[k],
                dst_ref=part(ref, me, size),
                send_sem=send_sem.at[a, d],
                recv_sem=recv_sem.at[a, me],
                device_id={"seq": k},
                device_id_type=MESH,
            )
            for a, values, ref, size in (
                (5, grad_out, out_ref, width),
                (6, read_out, read_ref, state),
            )
        ]

    def result_arrivals(d):
        peer = peers[d]
        return [
            pltpu.make_async_remote_copy(
                src_ref=values.at[peer],
                dst_ref=part(ref, peer, size),
                send_sem=send_sem.at[a, d],
                recv_sem=recv_sem.at[a, peer],
                device_id={"seq": peer},
                device_id_type=MESH,
            )
            for a, values, ref, size in (
                (5, grad_out, out_ref, width),
                (6, read_out, read_ref, state),
            )
        ]

    def back(i, _):
        k = partner(i)
        write = bs[k]
        ending = ends[k]
        grads = jnp.zeros((length, length), F32)
        for j in range(pairs):
            delta = half[k, :, span(j)]
            product = mm(delta, apart(xs[k, :, span(j)]), NT) * weights[k, j]
            grads = grads + product[:, :length] + product[:, length:]
            turned = mm(mix[k, j], delta, TN)
            out = jnp.where(left, turned[:length], turned[length:])
            out = out + pick(ending, j) * mm(write, carried_grad[k + 1, :, span(j)], NN)
            out = out + skip_pair(j) * y[k, :, span(j)]
            grad_out[k, :, span(j)] = out.astype(BF16)
        read_out[k] = (mm(grads.astype(BF16), write, NN) + read_part[k]).astype(BF16)

        @pl.when(i < n - 1)
        def _():
            for copy in results(i, k):
                copy.start()

        return 0

    lax.fori_loop(0, n, back, 0)

    last = [
        pltpu.make_async_copy(grad_out.at[me], part(out_ref, me, width), local_sem.at[5]),
        pltpu.make_async_copy(read_out.at[me], part(read_ref, me, state), local_sem.at[6]),
    ]
    for copy in last:
        copy.start()
    for d in range(reps - 1):
        rep_arrival(d).wait_recv()
    everything = sums[0]
    for r in range(1, reps):
        everything = everything + sums[r]
    gain_out[...] = everything[0:1]
    lane = lax.broadcasted_iota(jnp.int32, (width, lanes), 0)
    head = lax.broadcasted_iota(jnp.int32, (width, lanes), 1)
    members = jnp.where(lane // P_SIZE == head, 1.0, 0.0).astype(BF16)
    rest, skip = everything[1:2], jnp.zeros((1, lanes), F32)
    for _ in range(3):
        piece = rest.astype(BF16)
        skip = skip + mm(piece, members, NN)
        rest = rest - piece.astype(F32)
    skip_out[...] = skip
    for d in range(n - 1):
        for a in range(5):
            send(a, d).wait_send()
        for copy in results(d, peers[d]):
            copy.wait_send()
        for copy in result_arrivals(d):
            copy.wait_recv()
    for d in range(reps - 1):
        rep_send_copy(d).wait_send()
    for copy in last:
        copy.wait()


def by_groups(n, reps, mixer_in, write_proj, read_proj, dt_steps, decay_exp, norm_gain, skip_gain, out_grad):
    length, channels = mixer_in.shape[1:]
    width, state = channels // n, write_proj.shape[2] // n
    heads = width // P_SIZE
    pairs = heads // 2
    hbm = pl.BlockSpec(memory_space=pltpu.HBM)
    vmem = pl.BlockSpec(memory_space=pltpu.VMEM)
    smem = pl.BlockSpec(memory_space=pltpu.SMEM)
    wide, square = (n, length, width), (n, length, state)
    mixer_grad, read_grad, gain_grad, skip_grad = pl.pallas_call(
        functools.partial(grouped_kernel, n, reps),
        out_shape=(
            jax.ShapeDtypeStruct((length, channels), BF16),
            jax.ShapeDtypeStruct((length, n * state), BF16),
            jax.ShapeDtypeStruct((1, width), F32),
            jax.ShapeDtypeStruct((1, 2 * P_SIZE), F32),
        ),
        in_specs=[hbm, hbm, hbm, hbm, vmem, vmem, vmem, smem],
        out_specs=(hbm, hbm, vmem, vmem),
        scratch_shapes=[
            pltpu.VMEM(wide, BF16),
            pltpu.VMEM(wide, BF16),
            pltpu.VMEM(square, BF16),
            pltpu.VMEM(square, BF16),
            pltpu.VMEM((n, 2 * heads, length), F32),
            pltpu.VMEM((n, 2 * heads, length), F32),
            pltpu.VMEM((n, length, length), F32),
            pltpu.VMEM((n, length, length), F32),
            pltpu.VMEM((n, pairs, length, 2 * length), BF16),
            pltpu.VMEM((n, pairs, length, 2 * length), F32),
            pltpu.VMEM(wide, F32),
            pltpu.VMEM(wide, BF16),
            pltpu.VMEM((n, length, 2 * P_SIZE), F32),
            pltpu.VMEM((n + 1, state, width), BF16),
            pltpu.VMEM((n + 1, state, width), BF16),
            pltpu.VMEM(square, F32),
            pltpu.VMEM(wide, BF16),
            pltpu.VMEM(square, BF16),
            pltpu.VMEM((reps, 2, width), F32),
            pltpu.SemaphoreType.DMA((7, n - 1)),
            pltpu.SemaphoreType.DMA((7, n)),
            pltpu.SemaphoreType.DMA((7,)),
            pltpu.SemaphoreType.DMA((max(reps - 1, 1),)),
            pltpu.SemaphoreType.DMA((reps,)),
        ],
        compiler_params=pltpu.CompilerParams(
            collective_id=0, has_side_effects=True, vmem_limit_bytes=62 * 1024 * 1024
        ),
    )(
        mixer_in[0],
        write_proj[0],
        read_proj[0],
        out_grad[0],
        dt_steps[0].T,
        decay_exp[0].T,
        norm_gain.reshape(1, width),
        skip_gain,
    )
    return (mixer_grad[None], read_grad[None], gain_grad[0], skip_grad[0, :heads])


def solution(mesh):
    n, reps = mesh.shape["seq"], mesh.shape["rep"]

    def step(*args):
        batch, length = args[0].shape[:2]
        if n == G and batch == 1 and length == N and 2 * P_SIZE == N:
            return by_groups(n, reps, *args)
        return on_device(*args)

    in_specs = (
        P("rep", "seq", None),
        P("rep", "seq", None),
        P("rep", "seq", None),
        P("rep", "seq", None),
        P("rep", "seq", None),
        P("seq"),
        P("seq"),
        P("rep", "seq", None),
    )
    out_specs = (P("rep", "seq", None), P("rep", "seq", None), P("seq"), P("seq"))
    return jax.shard_map(
        step, mesh=mesh, in_specs=in_specs, out_specs=out_specs, check_vma=False
    )
```

```python
import functools

import jax
import jax.numpy as jnp
from jax import lax
from jax.experimental import pallas as pl
from jax.experimental.pallas import tpu as pltpu
from jax.sharding import PartitionSpec as P

MESH = pl.DeviceIdType.MESH
F32, BF16 = jnp.float32, jnp.bfloat16

H = 64
P_SIZE = 64
N = 128
G = 4
HG = 16


def entering(array, axis, combine, identity, reverse):
    devices, here = (lax.axis_size(axis), lax.axis_index(axis))
    everything = jax.tree.map(lambda part: lax.all_gather(part, axis), array)
    start = jax.tree.map(
        lambda part, zero: jnp.broadcast_to(jnp.asarray(zero, part.dtype), part.shape),
        array,
        identity,
    )

    def lap(k, before):
        at = devices - 1 - k if reverse else k
        reached = at > here if reverse else at < here
        new = combine(before, jax.tree.map(lambda part: part[at], everything))
        return jax.tree.map(lambda a, b: jnp.where(reached, a, b), new, before)

    return lax.fori_loop(0, devices, lap, start)


def contract(form, left, right):
    return jnp.einsum(form, left, right, preferred_element_type=jnp.float32)


def decay_weights(log_decay, step_size):
    length = log_decay.shape[2]
    causal = jnp.arange(length)[:, None] >= jnp.arange(length)[None, :]
    spread = jnp.where(causal, log_decay[:, :, :, None] - log_decay[:, :, None, :], 0.0)
    return jnp.where(causal, jnp.exp(spread), 0.0) * step_size[:, :, None, :]


def block_front(mixed, write, read, steps, decay):
    length = mixed.shape[3]
    exponents = jnp.transpose(decay).reshape(G, HG, 1, length)
    upto = jnp.arange(length)[:, None] >= jnp.arange(length)[None, :]
    log_decay = -(jnp.sum(jnp.where(upto, exponents, 0), axis=3).astype(jnp.float32) / 65536.0)
    step_size = jnp.transpose(steps).reshape(G, HG, length).astype(jnp.float32) / 16.0
    weights = decay_weights(log_decay, step_size)
    scores = contract("gnt,gns->gts", read, write)
    mixing = (scores[:, None] * weights).astype(jnp.bfloat16)
    inner_part = contract("gjts,gjps->gjpt", mixing, mixed)
    ending = jnp.exp(log_decay[:, :, -1:] - log_decay) * step_size
    weighted = (mixed.astype(jnp.float32) * ending[:, :, None, :]).astype(jnp.bfloat16)
    span_state = contract("gjps,gns->gjpn", weighted, write).astype(jnp.bfloat16)
    block_decay = jnp.exp(log_decay[:, :, -1]).astype(jnp.bfloat16)
    readout = jnp.exp(log_decay)
    return (log_decay, step_size, mixing, inner_part, ending, span_state, block_decay, readout)


def block_middle(mixed, read, skip_full, gain_full, upstream, inner_part, readout, carried):
    mixed_wide = mixed.astype(jnp.float32)
    mixer_out = (
        inner_part
        + readout[:, :, None, :] * contract("gnt,gjpn->gjpt", read, carried)
        + skip_full[:, :, None, None] * mixed_wide
    )
    inverse = lax.rsqrt(jnp.mean(mixer_out * mixer_out, axis=(1, 2), keepdims=True) + 1e-05)
    normed = mixer_out * inverse
    upstream_wide = upstream.astype(jnp.float32)
    normed_grad = upstream_wide * gain_full[:, :, :, None]
    gain_part = jnp.sum(upstream_wide * normed, axis=3)
    delta_wide = inverse * (
        normed_grad - normed * jnp.mean(normed_grad * normed, axis=(1, 2), keepdims=True)
    )
    skip_part = jnp.sum(delta_wide * mixed_wide, axis=(2, 3))
    delta_half = delta_wide.astype(jnp.bfloat16)
    scaled_delta = (delta_wide * readout[:, :, None, :]).astype(jnp.bfloat16)
    state_grad = contract("gjpt,gnt->gjpn", scaled_delta, read).astype(jnp.bfloat16)
    read_part = contract("gjpt,gjpn->gnt", scaled_delta, carried)
    return (delta_wide, delta_half, state_grad, read_part, gain_part, skip_part)


def block_back(
    mixed,
    write,
    skip_full,
    log_decay,
    step_size,
    mixing,
    ending,
    delta_wide,
    delta_half,
    read_part,
    carried_grad,
):
    weights = decay_weights(log_decay, step_size)
    mix_grad = contract("gjpt,gjps->gjts", delta_half, mixed)
    score_grad = jnp.sum(mix_grad * weights, axis=1).astype(jnp.bfloat16)
    read_grad = contract("gts,gns->gnt", score_grad, write) + read_part
    mixer_grad = contract("gjts,gjpt->gjps", mixing, delta_half)
    mixer_grad = mixer_grad + ending[:, :, None, :] * contract(
        "gns,gjpn->gjps", write, carried_grad
    )
    mixer_grad = mixer_grad + skip_full[:, :, None, None] * delta_wide
    return (mixer_grad.astype(jnp.bfloat16), read_grad.astype(jnp.bfloat16))


def forward_join(earlier, later):
    decay_early, state_early = earlier
    decay_late, state_late = later
    joined = (decay_early.astype(jnp.float32) * decay_late.astype(jnp.float32)).astype(jnp.bfloat16)
    state = (
        decay_late.astype(jnp.float32)[..., None, None] * state_early.astype(jnp.float32)
        + state_late.astype(jnp.float32)
    ).astype(jnp.bfloat16)
    return (joined, state)


def backward_join(earlier, later):
    decay_early, grad_early = earlier
    decay_late, grad_late = later
    joined = (decay_early.astype(jnp.float32) * decay_late.astype(jnp.float32)).astype(jnp.bfloat16)
    grads = (
        grad_late.astype(jnp.float32)
        + decay_late.astype(jnp.float32)[..., None, None] * grad_early.astype(jnp.float32)
    ).astype(jnp.bfloat16)
    return (joined, grads)


def neutral(block_decay, span_state):
    return (jnp.ones(block_decay.shape, jnp.bfloat16), jnp.zeros(span_state.shape, jnp.bfloat16))


def states_whole(block_decay, span_state):
    return entering(
        (block_decay, span_state), "seq", forward_join, neutral(block_decay, span_state), False
    )[1]


def grads_whole(block_decay, state_grad):
    return entering(
        (block_decay, state_grad), "seq", backward_join, neutral(block_decay, state_grad), True
    )[1]


def on_device(mixer_in, write_proj, read_proj, dt_steps, decay_exp, norm_gain, skip_gain, out_grad):
    length = mixer_in.shape[1]
    mixed = jnp.transpose(mixer_in[0].reshape(length, G, HG, P_SIZE), (1, 2, 3, 0))
    upstream = jnp.transpose(out_grad[0].reshape(length, G, HG, P_SIZE), (1, 2, 3, 0))
    write = jnp.transpose(write_proj[0].reshape(length, G, N), (1, 2, 0))
    read = jnp.transpose(read_proj[0].reshape(length, G, N), (1, 2, 0))
    gain_whole, skip_whole = (
        lax.all_gather(norm_gain, "seq", axis=0, tiled=True),
        lax.all_gather(skip_gain, "seq", axis=0, tiled=True),
    )
    gain_full = gain_whole.reshape(G, HG, P_SIZE)
    skip_full = skip_whole.reshape(G, HG)
    log_decay, step_size, mixing, inner_part, ending, span_state, block_decay, readout = (
        block_front(mixed, write, read, dt_steps[0], decay_exp[0])
    )
    carried = states_whole(block_decay, span_state)
    delta_wide, delta_half, state_grad, read_part, gain_part, skip_part = block_middle(
        mixed, read, skip_full, gain_full, upstream, inner_part, readout, carried
    )
    carried_grad = grads_whole(block_decay, state_grad)
    mixer_grad, read_grad = block_back(
        mixed,
        write,
        skip_full,
        log_decay,
        step_size,
        mixing,
        ending,
        delta_wide,
        delta_half,
        read_part,
        carried_grad,
    )
    gain_flat = gain_part.reshape(H * P_SIZE)
    skip_flat = skip_part.reshape(H)
    gain_share, skip_share = (
        lax.psum_scatter(gain_flat, "seq", scatter_dimension=0, tiled=True),
        lax.psum_scatter(skip_flat, "seq", scatter_dimension=0, tiled=True),
    )
    gain_piece, skip_piece = lax.psum((gain_share, skip_share), "rep")
    mixer_rows = jnp.transpose(mixer_grad, (3, 0, 1, 2)).reshape(1, length, H * P_SIZE)
    read_rows = jnp.transpose(read_grad, (2, 0, 1)).reshape(1, length, G * N)
    return (mixer_rows, read_rows, gain_piece, skip_piece)


def mm(a, b, dims):
    return lax.dot_general(a, b, (dims, ((), ())), preferred_element_type=F32)


NN, NT, TN = ((1,), (0,)), ((1,), (1,)), ((0,), (0,))


def grouped_kernel(
    n,
    reps,
    x_ref,
    b_ref,
    c_ref,
    u_ref,
    steps_ref,
    decay_ref,
    gain_ref,
    skip_ref,
    out_ref,
    read_ref,
    gain_out,
    skip_out,
    xs,
    us,
    bs,
    cs,
    table_out,
    table,
    cols,
    ends,
    mix,
    weights,
    y,
    half,
    inv,
    carried,
    carried_grad,
    read_part,
    grad_out,
    read_out,
    sums,
    send_sem,
    recv_sem,
    local_sem,
    rep_send,
    rep_recv,
):
    me, my_rep = lax.axis_index("seq"), lax.axis_index("rep")
    length, width, state = xs.shape[1], xs.shape[2], bs.shape[2]
    heads = table.shape[1] // 2
    pairs = width // (2 * P_SIZE)
    lanes = 2 * P_SIZE
    swap = lax.rem(my_rep, 2)

    def partner(i):
        step = lax.rem(i + 1, n)
        minor, major = lax.rem(step, 2), step // 2
        minor, major = minor + swap * (major - minor), major + swap * (minor - major)
        return lax.rem(me + minor, 2) + 2 * lax.rem(me // 2 + major, 2)

    peers = [partner(d) for d in range(n - 1)]
    rep_peers = [lax.rem(my_rep + d, reps) for d in range(1, reps)]

    barrier = pltpu.get_barrier_semaphore()
    for peer in peers:
        pl.semaphore_signal(barrier, inc=1, device_id={"seq": peer}, device_id_type=MESH)
    for peer in rep_peers:
        pl.semaphore_signal(barrier, inc=1, device_id={"rep": peer}, device_id_type=MESH)

    row = lax.broadcasted_iota(jnp.int32, (length, length), 0)
    col = lax.broadcasted_iota(jnp.int32, (length, length), 1)
    causal = row >= col
    left = lax.broadcasted_iota(jnp.int32, (length, lanes), 1) < P_SIZE
    left_row = lax.broadcasted_iota(jnp.int32, (1, lanes), 1) < P_SIZE

    triangle = jnp.where(row <= col, 1.0, 0.0).astype(BF16)
    decay = decay_ref[...]
    high = (decay >> 8).astype(F32).astype(BF16)
    low = (decay & 255).astype(F32).astype(BF16)
    total = mm(high, triangle, NN) * 256.0 + mm(low, triangle, NN)
    log_decay, step_size = total * (-1.0 / 65536.0), steps_ref[...].astype(F32) / 16.0
    for g in range(n):
        table_out[g, :heads] = log_decay[g * heads : (g + 1) * heads]
        table_out[g, heads:] = step_size[g * heads : (g + 1) * heads]

    def part(ref, g, size):
        return ref.at[:, pl.ds(pl.multiple_of(g * size, size), size)]

    def source(a, g):
        if a == 0:
            return table_out.at[g]
        return part((x_ref, b_ref, c_ref, u_ref)[a - 1], g, (width, state, state, width)[a - 1])

    target = (table, xs, bs, cs, us)

    def send(a, d):
        return pltpu.make_async_remote_copy(
            src_ref=source(a, peers[d]),
            dst_ref=target[a].at[me],
            send_sem=send_sem.at[a, d],
            recv_sem=recv_sem.at[a, me],
            device_id={"seq": peers[d]},
            device_id_type=MESH,
        )

    def arrival(a, d):
        return pltpu.make_async_remote_copy(
            src_ref=source(a, peers[d]),
            dst_ref=target[a].at[peers[d]],
            send_sem=send_sem.at[a, d],
            recv_sem=recv_sem.at[a, peers[d]],
            device_id={"seq": peers[d]},
            device_id_type=MESH,
        )

    own = [
        pltpu.make_async_copy(source(a, me), target[a].at[me], local_sem.at[a]) for a in range(5)
    ]
    for copy in own:
        copy.start()
    pl.semaphore_wait(barrier, n - 1 + reps - 1)
    for a in (0, 2, 3, 1):
        for d in range(n - 1):
            send(a, d).start()
    for copy in own:
        copy.wait()
    for a in (0, 2, 3):
        for d in range(n - 1):
            arrival(a, d).wait_recv()

    def span(j):
        return slice(j * lanes, (j + 1) * lanes)

    def pick(values, j):
        return jnp.where(left, values[:, 2 * j : 2 * j + 1], values[:, 2 * j + 1 : 2 * j + 2])

    def pick_row(values, j):
        return jnp.where(left_row, values[:, 2 * j : 2 * j + 1], values[:, 2 * j + 1 : 2 * j + 2])

    def skip_pair(j):
        return jnp.where(left_row, skip_ref[2 * j], skip_ref[2 * j + 1])

    def apart(values):
        zero = jnp.zeros_like(values)
        return jnp.concatenate([jnp.where(left, values, zero), jnp.where(left, zero, values)], axis=0)

    def closing(k):
        return jnp.exp(cols[k][length - 1 :, :]).astype(BF16).astype(F32)

    carried[0] = jnp.zeros(carried.shape[1:], BF16)
    carried_grad[n] = jnp.zeros(carried_grad.shape[1:], BF16)

    def front(k, _):
        tab = table[k]
        copies = length // (2 * heads)
        c = jnp.concatenate([tab] * copies, axis=0).T
        swapped = jnp.concatenate([tab[heads:], tab[:heads]] * copies, axis=0).T
        cols[k] = c
        ends[k] = jnp.exp(c[length - 1 :, :] - c) * swapped
        scores = mm(cs[k], bs[k], NT)
        for j in range(pairs):
            for e in range(2):
                h = 2 * j + e
                spread = jnp.where(causal, c[:, h : h + 1] - tab[h : h + 1, :], -1e30)
                w = jnp.exp(spread) * tab[heads + h : heads + h + 1, :]
                weights[k, j, :, e * length : (e + 1) * length] = w
                mix[k, j, :, e * length : (e + 1) * length] = (scores * w).astype(BF16)
        return 0

    lax.fori_loop(0, n, front, 0)

    for d in range(n - 1):
        send(4, d).start()
    def await_block(a, k):
        @pl.when(k != me)
        def _():
            pltpu.make_async_remote_copy(
                src_ref=target[a].at[k],
                dst_ref=target[a].at[k],
                send_sem=send_sem.at[a, 0],
                recv_sem=recv_sem.at[a, k],
                device_id={"seq": k},
                device_id_type=MESH,
            ).wait_recv()

    def forward(k, _):
        await_block(1, k)
        ending = ends[k]
        readout = jnp.exp(cols[k])
        block_decay = closing(k)
        write, read = bs[k], cs[k]
        squares = jnp.zeros((length, lanes), F32)
        for j in range(pairs):
            x = xs[k, :, span(j)]
            wide = x.astype(F32)
            before = carried[k, :, span(j)]
            out = mm(mix[k, j], apart(x), NN)
            out = out + pick(readout, j) * mm(read, before, NN) + skip_pair(j) * wide
            y[k, :, span(j)] = out
            squares = squares + out * out
            weighted = (wide * pick(ending, j)).astype(BF16)
            grown = mm(write, weighted, TN).astype(BF16).astype(F32)
            carried[k + 1, :, span(j)] = (
                pick_row(block_decay, j) * before.astype(F32) + grown
            ).astype(BF16)
        mean = jnp.sum(squares, axis=1, keepdims=True) / width
        inv[k] = jnp.broadcast_to(lax.rsqrt(mean + 1e-05), inv.shape[1:])
        return 0

    lax.fori_loop(0, n, forward, 0)

    sums[my_rep] = jnp.zeros(sums.shape[1:], F32)

    def middle(i, _):
        k = n - 1 - i
        await_block(4, k)
        inverse = inv[k]
        readout = jnp.exp(cols[k])
        block_decay = closing(k)
        read = cs[k]
        inner = jnp.zeros((length, lanes), F32)
        for j in range(pairs):
            up = us[k, :, span(j)].astype(F32)
            normed = y[k, :, span(j)] * inverse
            product = up * normed
            inner = inner + product * gain_ref[:, span(j)]
            sums[my_rep, 0:1, span(j)] += jnp.sum(product, axis=0, keepdims=True)
        mean = jnp.sum(inner, axis=1, keepdims=True) / width
        kept = jnp.zeros((length, state), F32)
        for j in range(pairs):
            up = us[k, :, span(j)].astype(F32)
            normed = y[k, :, span(j)] * inverse
            delta = inverse * (up * gain_ref[:, span(j)] - normed * mean)
            y[k, :, span(j)] = delta
            half[k, :, span(j)] = delta.astype(BF16)
            wide = xs[k, :, span(j)].astype(F32)
            sums[my_rep, 1:2, span(j)] += jnp.sum(delta * wide, axis=0, keepdims=True)
            scaled = (delta * pick(readout, j)).astype(BF16)
            state_grad = mm(read, scaled, TN).astype(BF16).astype(F32)
            kept = kept + mm(scaled, carried[k, :, span(j)], NT)
            later = carried_grad[k + 1, :, span(j)].astype(F32)
            carried_grad[k, :, span(j)] = (
                state_grad + pick_row(block_decay, j) * later
            ).astype(BF16)
        read_part[k] = kept
        return 0

    lax.fori_loop(0, n, middle, 0)

    def rep_send_copy(d):
        return pltpu.make_async_remote_copy(
            src_ref=sums.at[my_rep],
            dst_ref=sums.at[my_rep],
            send_sem=rep_send.at[d],
            recv_sem=rep_recv.at[my_rep],
            device_id={"rep": rep_peers[d]},
            device_id_type=MESH,
        )

    def rep_arrival(d):
        return pltpu.make_async_remote_copy(
            src_ref=sums.at[my_rep],
            dst_ref=sums.at[rep_peers[d]],
            send_sem=rep_send.at[d],
            recv_sem=rep_recv.at[rep_peers[d]],
            device_id={"rep": rep_peers[d]},
            device_id_type=MESH,
        )

    for d in range(reps - 1):
        rep_send_copy(d).start()

    def results(d, k):
        return [
            pltpu.make_async_remote_copy(
                src_ref=values.at[k],
                dst_ref=part(ref, me, size),
                send_sem=send_sem.at[a, d],
                recv_sem=recv_sem.at[a, me],
                device_id={"seq": k},
                device_id_type=MESH,
            )
            for a, values, ref, size in (
                (5, grad_out, out_ref, width),
                (6, read_out, read_ref, state),
            )
        ]

    def result_arrivals(d):
        peer = peers[d]
        return [
            pltpu.make_async_remote_copy(
                src_ref=values.at[peer],
                dst_ref=part(ref, peer, size),
                send_sem=send_sem.at[a, d],
                recv_sem=recv_sem.at[a, peer],
                device_id={"seq": peer},
                device_id_type=MESH,
            )
            for a, values, ref, size in (
                (5, grad_out, out_ref, width),
                (6, read_out, read_ref, state),
            )
        ]

    def back(i, _):
        k = partner(i)
        write = bs[k]
        ending = ends[k]
        grads = jnp.zeros((length, length), F32)
        for j in range(pairs):
            delta = half[k, :, span(j)]
            product = mm(delta, apart(xs[k, :, span(j)]), NT) * weights[k, j]
            grads = grads + product[:, :length] + product[:, length:]
            turned = mm(mix[k, j], delta, TN)
            out = jnp.where(left, turned[:length], turned[length:])
            out = out + pick(ending, j) * mm(write, carried_grad[k + 1, :, span(j)], NN)
            out = out + skip_pair(j) * y[k, :, span(j)]
            grad_out[k, :, span(j)] = out.astype(BF16)
        read_out[k] = (mm(grads.astype(BF16), write, NN) + read_part[k]).astype(BF16)

        @pl.when(i < n - 1)
        def _():
            for copy in results(i, k):
                copy.start()

        return 0

    lax.fori_loop(0, n, back, 0)

    last = [
        pltpu.make_async_copy(grad_out.at[me], part(out_ref, me, width), local_sem.at[5]),
        pltpu.make_async_copy(read_out.at[me], part(read_ref, me, state), local_sem.at[6]),
    ]
    for copy in last:
        copy.start()
    for d in range(reps - 1):
        rep_arrival(d).wait_recv()
    everything = sums[0]
    for r in range(1, reps):
        everything = everything + sums[r]
    gain_out[...] = everything[0:1]
    lane = lax.broadcasted_iota(jnp.int32, (width, lanes), 0)
    head = lax.broadcasted_iota(jnp.int32, (width, lanes), 1)
    members = jnp.where(lane // P_SIZE == head, 1.0, 0.0).astype(BF16)
    rest, skip = everything[1:2], jnp.zeros((1, lanes), F32)
    for _ in range(3):
        piece = rest.astype(BF16)
        skip = skip + mm(piece, members, NN)
        rest = rest - piece.astype(F32)
    skip_out[...] = skip
    for d in range(n - 1):
        for a in range(5):
            send(a, d).wait_send()
        for copy in results(d, peers[d]):
            copy.wait_send()
        for copy in result_arrivals(d):
            copy.wait_recv()
    for d in range(reps - 1):
        rep_send_copy(d).wait_send()
    for copy in last:
        copy.wait()


def by_groups(n, reps, mixer_in, write_proj, read_proj, dt_steps, decay_exp, norm_gain, skip_gain, out_grad):
    length, channels = mixer_in.shape[1:]
    width, state = channels // n, write_proj.shape[2] // n
    heads = width // P_SIZE
    pairs = heads // 2
    hbm = pl.BlockSpec(memory_space=pltpu.HBM)
    vmem = pl.BlockSpec(memory_space=pltpu.VMEM)
    smem = pl.BlockSpec(memory_space=pltpu.SMEM)
    wide, square = (n, length, width), (n, length, state)
    mixer_grad, read_grad, gain_grad, skip_grad = pl.pallas_call(
        functools.partial(grouped_kernel, n, reps),
        out_shape=(
            jax.ShapeDtypeStruct((length, channels), BF16),
            jax.ShapeDtypeStruct((length, n * state), BF16),
            jax.ShapeDtypeStruct((1, width), F32),
            jax.ShapeDtypeStruct((1, 2 * P_SIZE), F32),
        ),
        in_specs=[hbm, hbm, hbm, hbm, vmem, vmem, vmem, smem],
        out_specs=(hbm, hbm, vmem, vmem),
        scratch_shapes=[
            pltpu.VMEM(wide, BF16),
            pltpu.VMEM(wide, BF16),
            pltpu.VMEM(square, BF16),
            pltpu.VMEM(square, BF16),
            pltpu.VMEM((n, 2 * heads, length), F32),
            pltpu.VMEM((n, 2 * heads, length), F32),
            pltpu.VMEM((n, length, length), F32),
            pltpu.VMEM((n, length, length), F32),
            pltpu.VMEM((n, pairs, length, 2 * length), BF16),
            pltpu.VMEM((n, pairs, length, 2 * length), F32),
            pltpu.VMEM(wide, F32),
            pltpu.VMEM(wide, BF16),
            pltpu.VMEM((n, length, 2 * P_SIZE), F32),
            pltpu.VMEM((n + 1, state, width), BF16),
            pltpu.VMEM((n + 1, state, width), BF16),
            pltpu.VMEM(square, F32),
            pltpu.VMEM(wide, BF16),
            pltpu.VMEM(square, BF16),
            pltpu.VMEM((reps, 2, width), F32),
            pltpu.SemaphoreType.DMA((7, n - 1)),
            pltpu.SemaphoreType.DMA((7, n)),
            pltpu.SemaphoreType.DMA((7,)),
            pltpu.SemaphoreType.DMA((max(reps - 1, 1),)),
            pltpu.SemaphoreType.DMA((reps,)),
        ],
        compiler_params=pltpu.CompilerParams(
            collective_id=0, has_side_effects=True, vmem_limit_bytes=62 * 1024 * 1024
        ),
    )(
        mixer_in[0],
        write_proj[0],
        read_proj[0],
        out_grad[0],
        dt_steps[0].T,
        decay_exp[0].T,
        norm_gain.reshape(1, width),
        skip_gain,
    )
    return (mixer_grad[None], read_grad[None], gain_grad[0], skip_grad[0, :heads])


def solution(mesh):
    n, reps = mesh.shape["seq"], mesh.shape["rep"]

    def step(*args):
        batch, length = args[0].shape[:2]
        if n == G and batch == 1 and length == N and 2 * P_SIZE == N:
            return by_groups(n, reps, *args)
        return on_device(*args)

    in_specs = (
        P("rep", "seq", None),
        P("rep", "seq", None),
        P("rep", "seq", None),
        P("rep", "seq", None),
        P("rep", "seq", None),
        P("seq"),
        P("seq"),
        P("rep", "seq", None),
    )
    out_specs = (P("rep", "seq", None), P("rep", "seq", None), P("seq"), P("seq"))
    return jax.shard_map(
        step, mesh=mesh, in_specs=in_specs, out_specs=out_specs, check_vma=False
    )
```
